32 devices in a mesh: dp: 8 (over y, x, core), context: 4 (over z).
Axes of the slice: x: 2, y: 2, z: 4, core: 2. Of those that a mesh axis runs over, the one named last changes fastest.
Arguments:
- residual_in: bfloat16 [8, 512, 4096], P('dp', 'context'), may hold values from -6 to 6
- residual_tangent: bfloat16 [8, 512, 4096], P('dp', 'context'), may hold values from -6 to 6
- queries: bfloat16 [8, 512, 4096], P('dp', 'context'), may hold values from -32 to 32, as said below
- key_rows: bfloat16 [8, 512, 4096], P('dp', 'context'), may hold values from -8 to 8
- value_rows: bfloat16 [8, 512, 4096], P('dp', 'context'), may hold values from -6 to 6
- query_tangent: bfloat16 [8, 512, 4096], P('dp', 'context'), may hold values from -6 to 6
- key_tangent: bfloat16 [8, 512, 4096], P('dp', 'context'), may hold values from -6 to 6
- value_tangent: bfloat16 [8, 512, 4096], P('dp', 'context'), may hold values from -6 to 6
- time_features: float32 [8, 4096], P('dp'), may hold values from -5 to 5
- time_tangent: float32 [8, 4096], P('dp'), may hold values from -5 to 5
- time_weight: bfloat16 [4096, 12288], P('dp', 'context'), may hold values from -0.09375 to 0.09375
- block_modulation: float32 [3, 4096], replicated, may hold values from -3 to 3
Outputs:
- normed: bfloat16 [8, 512, 4096], P('dp', 'context')
- normed_tangent: bfloat16 [8, 512, 4096], P('dp', 'context')
The draws below stay inside these ranges and needn't reach their ends.
Inputs may be any that keep to these rules, and one draw needn't show every extreme that they name: `queries`: query entries.
All inputs are finite; a program needn't handle non-finite values.
Results may differ from the reference program's by a relative error of at most 0.0046.
Values may be sent and summed in bfloat16 or wider, within the bound.
A program may use at most 128 MiB of HBM per device.

```python
import jax
import jax.numpy as jnp
from jax import lax

HEADS = 32
HEAD = 128
D = 4096
TOKENS = 512
CLIPS = 8


def draw_key_rows(key, part):
    key = jax.random.fold_in(key, 11)
    return jax.random.normal(key, (CLIPS, TOKENS, D), jnp.float32).astype(jnp.bfloat16)


def draw_queries(key, part):
    key = jax.random.fold_in(key, 12)
    return jax.random.normal(key, (CLIPS, TOKENS, D), jnp.float32).astype(jnp.bfloat16)


def block_levels(stream_key, shape, split, least, largest):
    gain = 1.0
    for axis_at, blocks in split:
        heights = jax.random.uniform(jax.random.fold_in(jax.random.fold_in(stream_key, 6), axis_at), (blocks,), jnp.float32, least / len(split), largest / len(split))
        gain = gain * jnp.repeat(jnp.exp(heights), shape[axis_at] // blocks).reshape((-1,) + (1,) * (len(shape) - 1 - axis_at))
    return gain


def gaussian(own_key, shape, width, most, cuts=(), kind=jnp.bfloat16):
    result = width * jax.random.normal(own_key, shape, jnp.float32)
    if cuts:
        result = result * block_levels(own_key, shape, cuts, -0.22, 0.18)
    return jnp.clip(result, -most, most).astype(kind)


def setup_inputs(seed: int = 0) -> dict:
    streams_of = jax.random.split(jax.random.key(seed), 13)
    residual_in = gaussian(streams_of[0], (CLIPS, TOKENS, D), 1.0, 6.0, ((0, 8), (1, 4)))
    residual_tangent = gaussian(streams_of[1], (CLIPS, TOKENS, D), 1.0, 6.0, ((0, 8), (1, 4)))
    queries = draw_queries(jax.random.fold_in(streams_of[12], 71), 0)
    key_rows = draw_key_rows(jax.random.fold_in(streams_of[12], 71), 0)
    value_rows = gaussian(streams_of[4], (CLIPS, TOKENS, D), 1.0, 6.0, ((0, 8), (1, 4)))
    query_tangent = gaussian(streams_of[5], (CLIPS, TOKENS, D), 1.0, 6.0, ((0, 8), (1, 4)))
    key_tangent = gaussian(streams_of[6], (CLIPS, TOKENS, D), 1.0, 6.0, ((0, 8), (1, 4)))
    value_tangent = gaussian(streams_of[7], (CLIPS, TOKENS, D), 1.0, 6.0, ((0, 8), (1, 4)))
    time_features = gaussian(streams_of[8], (CLIPS, D), 1.0, 5.0, ((0, 8),), jnp.float32)
    time_tangent = gaussian(streams_of[9], (CLIPS, D), 1.0, 5.0, ((0, 8),), jnp.float32)
    time_weight = gaussian(streams_of[10], (D, 3 * D), D ** -0.5, 0.09375, ((0, 8), (1, 4)))
    block_modulation = gaussian(streams_of[11], (3, D), 0.5, 3.0, (), jnp.float32)
    return dict(residual_in=residual_in, residual_tangent=residual_tangent, queries=queries, key_rows=key_rows, value_rows=value_rows, query_tangent=query_tangent, key_tangent=key_tangent, value_tangent=value_tangent, time_features=time_features, time_tangent=time_tangent, time_weight=time_weight, block_modulation=block_modulation)


def head_attention(query, keyset, values, query_dot, key_dot, value_dot):
    length = query.shape[0]
    size = min(512, length)
    count = length // size
    factor = 1.0 / query.shape[1] ** 0.5

    def one_block(pair):
        block_q, block_dq = pair
        scores = jnp.dot(block_q, keyset.T, preferred_element_type=jnp.float32) * factor
        score_dot = (jnp.dot(block_dq, keyset.T, preferred_element_type=jnp.float32) + jnp.dot(block_q, key_dot.T, preferred_element_type=jnp.float32)) * factor
        top = lax.optimization_barrier(jnp.max(scores, axis=1, keepdims=True))
        expo = jnp.exp(scores - top)
        probs = expo / lax.optimization_barrier(jnp.sum(expo, axis=1, keepdims=True))
        probs_low = probs.astype(jnp.bfloat16)
        weighted = probs * score_dot
        centre = lax.optimization_barrier(jnp.sum(weighted, axis=1, keepdims=True))
        weighted_low = weighted.astype(jnp.bfloat16)
        attended = jnp.dot(probs_low, values, preferred_element_type=jnp.float32)
        tangent = jnp.dot(probs_low, value_dot, preferred_element_type=jnp.float32) + jnp.dot(weighted_low, values, preferred_element_type=jnp.float32) - centre * attended
        return (attended.astype(jnp.bfloat16), tangent.astype(jnp.bfloat16))
    shaped = (query.reshape(count, size, -1), query_dot.reshape(count, size, -1))
    attended, tangent = lax.map(one_block, shaped)
    return (attended.reshape(length, -1), tangent.reshape(length, -1))

def prepare(resid, resid_dot, attended, attended_dot, mods, mods_dot):
    hidden_state = resid.astype(jnp.float32) + mods[0] * attended.astype(jnp.float32)
    hidden_tangent = resid_dot.astype(jnp.float32) + mods[0] * attended_dot.astype(jnp.float32) + mods_dot[0] * attended.astype(jnp.float32)
    centered = hidden_state - lax.optimization_barrier(jnp.mean(hidden_state, axis=1, keepdims=True))
    inverse = lax.rsqrt(lax.optimization_barrier(jnp.mean(centered * centered, axis=1, keepdims=True)) + 1e-06)
    unit = centered * inverse
    unit_dot = (hidden_tangent - lax.optimization_barrier(jnp.mean(hidden_tangent, axis=1, keepdims=True)) - unit * lax.optimization_barrier(jnp.mean(unit * hidden_tangent, axis=1, keepdims=True))) * inverse
    normed = (unit * (1.0 + mods[2]) + mods[1]).astype(jnp.bfloat16)
    normed_dot = (unit_dot * (1.0 + mods[2]) + unit * mods_dot[2] + mods_dot[1]).astype(jnp.bfloat16)
    return (normed, normed_dot)

def split_heads(matrix):
    return matrix.reshape(matrix.shape[0], HEADS, HEAD).transpose(1, 0, 2)

def reference(residual_in, residual_tangent, queries, key_rows, value_rows, query_tangent, key_tangent, value_tangent, time_features, time_tangent, time_weight, block_modulation):
    act, act_dot = jax.jvp(jax.nn.silu, (time_features,), (time_tangent,))
    act = act.astype(jnp.bfloat16)
    act_dot = act_dot.astype(jnp.bfloat16)
    projected = jnp.dot(act, time_weight, preferred_element_type=jnp.float32)
    projected_dot = jnp.dot(act_dot, time_weight, preferred_element_type=jnp.float32)
    modulation = block_modulation[None] + projected.reshape(CLIPS, 3, D)
    modulation_dot = projected_dot.reshape(CLIPS, 3, D)

    def per_clip(items):
        resid, resid_dot, query, keyset, values, query_dot, key_dot, value_dot, mods, mods_dot = items
        heads = tuple((split_heads(matrix) for matrix in (query, keyset, values, query_dot, key_dot, value_dot)))
        attended, attended_dot = lax.map(lambda group: head_attention(*group), heads)
        length = query.shape[0]
        attended = attended.transpose(1, 0, 2).reshape(length, -1)
        attended_dot = attended_dot.transpose(1, 0, 2).reshape(length, -1)
        return prepare(resid, resid_dot, attended, attended_dot, mods, mods_dot)
    return lax.map(per_clip, (residual_in, residual_tangent, queries, key_rows, value_rows, query_tangent, key_tangent, value_tangent, modulation, modulation_dot))
```

```python
import functools
import math

import jax
import jax.numpy as jnp
from jax import lax
from jax.experimental import pallas as pl
from jax.experimental.pallas import tpu as pltpu
from jax.sharding import PartitionSpec as P

HEADS = 32
HEAD = 128
EPS = 1e-06
MESH = pl.DeviceIdType.MESH


def flip(index, mask):
    bit = 1
    while bit <= mask:
        if mask & bit:
            index = index + bit * (1 - 2 * lax.rem(index // bit, 2))
        bit *= 2
    return index


def kernel(
    n_ctx,
    n_dp,
    res_ref,
    rest_ref,
    q_ref,
    k_ref,
    v_ref,
    dq_ref,
    dk_ref,
    dv_ref,
    tf_ref,
    tt_ref,
    w_ref,
    bm_ref,
    out_ref,
    outt_ref,
    rbuf,
    obuf,
    ret,
    resv,
    wv,
    act_s,
    act_r,
    part_s,
    part_r,
    mod_s,
    mod_r,
    mods,
    outv,
    in_send,
    in_recv,
    own_sem,
    ret_send,
    ret_recv,
    act_send,
    act_recv,
    part_send,
    part_recv,
    mod_send,
    mod_recv,
    loc_sem,
    out_sem,
):
    heads, _, length, _ = rbuf.shape
    tokens = ret.shape[1]
    width = ret.shape[2]
    rows_w, cols_w = wv.shape
    me = lax.axis_index("context")
    clip = lax.axis_index("dp")
    masks = list(range(n_ctx - 1, 0, -1))
    steps = list(range(1, n_dp))
    sources = (q_ref, k_ref, v_ref, dq_ref, dk_ref, dv_ref)

    barrier = pltpu.get_barrier_semaphore()
    for mask in masks:
        pl.semaphore_signal(barrier, inc=1, device_id={"context": flip(me, mask)}, device_id_type=MESH)
    for step in steps:
        pl.semaphore_signal(barrier, inc=1, device_id={"dp": lax.rem(clip + step, n_dp)}, device_id_type=MESH)

    local = [
        pltpu.make_async_copy(w_ref, wv, loc_sem.at[0]),
        pltpu.make_async_copy(res_ref.at[0], resv.at[0], loc_sem.at[1]),
        pltpu.make_async_copy(rest_ref.at[0], resv.at[1], loc_sem.at[2]),
    ]
    local[0].start()

    def own_rows(owner):
        return pl.ds(pl.multiple_of(owner * tokens, tokens), tokens)

    mine = own_rows(me)
    pl.semaphore_wait(barrier, len(masks) + len(steps))

    def send_head(head, carry):
        for mask in masks:
            peer = flip(me, mask)
            at = pl.multiple_of((peer * heads + head) * HEAD, HEAD)
            for slot, source in enumerate(sources):
                pltpu.make_async_remote_copy(
                    src_ref=source.at[0, :, pl.ds(at, HEAD)],
                    dst_ref=rbuf.at[head, slot, mine, :],
                    send_sem=in_send.at[mask - 1],
                    recv_sem=in_recv.at[head, mask - 1],
                    device_id={"context": peer},
                    device_id_type=MESH,
                ).start()
        return carry

    lax.fori_loop(0, heads, send_head, 0)

    def own_head(head, carry):
        at = pl.multiple_of((me * heads + head) * HEAD, HEAD)
        for slot, source in enumerate(sources):
            pltpu.make_async_copy(
                source.at[0, :, pl.ds(at, HEAD)], rbuf.at[head, slot, mine, :], own_sem.at[head]
            ).start()
        return carry

    x = tf_ref[...]
    gate = 1.0 / (1.0 + jnp.exp(-x))
    act = x * gate
    act_dot = tt_ref[...] * (gate * (1.0 + x * (1.0 - gate)))
    act_s[...] = jnp.zeros_like(act_s)
    for step in range(n_dp):
        act_s[step, 0:1, :] = act[:, step * rows_w : (step + 1) * rows_w]
        act_s[step, 1:2, :] = act_dot[:, step * rows_w : (step + 1) * rows_w]
    act_copies = []
    for step in steps:
        peer = lax.rem(clip + step, n_dp)
        copy = pltpu.make_async_remote_copy(
            src_ref=act_s.at[peer],
            dst_ref=act_r.at[clip],
            send_sem=act_send.at[step - 1],
            recv_sem=act_recv.at[step - 1],
            device_id={"dp": peer},
            device_id_type=MESH,
        )
        copy.start()
        act_copies.append(copy)
    lax.fori_loop(0, heads, own_head, 0)
    local[1].start()
    local[2].start()
    act_r[clip] = act_s[clip]
    for copy in act_copies:
        copy.wait()
    local[0].wait()
    lhs = act_r[...].reshape(n_dp * 8, rows_w).astype(jnp.bfloat16)
    tile = cols_w // 6

    for t in range(6):
        cols = slice(t * tile, (t + 1) * tile)
        prod = jnp.dot(lhs, wv[:, cols], preferred_element_type=jnp.float32)
        part_s[:, :, cols] = prod.reshape(n_dp, 8, tile)
    part_copies = []
    for step in steps:
        peer = lax.rem(clip + step, n_dp)
        copy = pltpu.make_async_remote_copy(
            src_ref=part_s.at[peer],
            dst_ref=part_r.at[clip],
            send_sem=part_send.at[step - 1],
            recv_sem=part_recv.at[step - 1],
            device_id={"dp": peer},
            device_id_type=MESH,
        )
        copy.start()
        part_copies.append(copy)
    part_r[clip] = part_s[clip]
    for copy in part_copies:
        copy.wait()
    total = part_r[0]
    for step in steps:
        total = total + part_r[step]
    quarter = cols_w // 4
    for piece in range(4):
        mod_s[2 * piece : 2 * piece + 2, :] = total[0:2, piece * quarter : (piece + 1) * quarter]
    mod_copies = []
    for mask in masks:
        copy = pltpu.make_async_remote_copy(
            src_ref=mod_s,
            dst_ref=mod_r.at[me],
            send_sem=mod_send.at[mask - 1],
            recv_sem=mod_recv.at[mask - 1],
            device_id={"context": flip(me, mask)},
            device_id_type=MESH,
        )
        copy.start()
        mod_copies.append(copy)
    mod_r[me] = mod_s[...]

    factor = 1.0 / HEAD**0.5
    block = min(256, length)

    def one_head(head, carry):
        pltpu.make_async_copy(rbuf.at[head, :, mine, :], rbuf.at[head, :, mine, :], own_sem.at[head]).wait()
        for mask in masks:
            theirs = rbuf.at[head, :, own_rows(flip(me, mask)), :]
            pltpu.make_async_copy(theirs, theirs, in_recv.at[head, mask - 1]).wait()

        def one_block(index, carry):
            rows = pl.ds(pl.multiple_of(index * block, block), block)
            query = rbuf[head, 0, rows, :]
            query_dot = rbuf[head, 3, rows, :]
            keyset = rbuf[head, 1]
            key_dot = rbuf[head, 4]
            values = rbuf[head, 2]
            value_dot = rbuf[head, 5]
            last = (((1,), (1,)), ((), ()))
            scores = lax.dot_general(query, keyset, last, preferred_element_type=jnp.float32) * factor
            score_dot = (
                lax.dot_general(
                    jnp.concatenate([query_dot, query], axis=1),
                    jnp.concatenate([keyset, key_dot], axis=1),
                    last,
                    preferred_element_type=jnp.float32,
                )
                * factor
            )
            top = jnp.max(scores, axis=1, keepdims=True)
            expo = jnp.exp(scores - top)
            probs = expo * (1.0 / jnp.sum(expo, axis=1, keepdims=True))
            probs_low = probs.astype(jnp.bfloat16)
            weighted = probs * score_dot
            centre = jnp.sum(weighted, axis=1, keepdims=True)
            weighted_low = weighted.astype(jnp.bfloat16)
            both = jnp.dot(
                probs_low, jnp.concatenate([values, value_dot], axis=1), preferred_element_type=jnp.float32
            )
            attended = both[:, :HEAD]
            tangent = (
                both[:, HEAD:]
                + jnp.dot(weighted_low, values, preferred_element_type=jnp.float32)
                - centre * attended
            )
            obuf[head, 0, rows, :] = attended.astype(jnp.bfloat16)
            obuf[head, 1, rows, :] = tangent.astype(jnp.bfloat16)
            return carry

        lax.fori_loop(0, length // block, one_block, 0)
        columns = pl.ds(pl.multiple_of((me * heads + head) * HEAD, HEAD), HEAD)
        for mask in masks:
            peer = flip(me, mask)
            pltpu.make_async_remote_copy(
                src_ref=obuf.at[head, :, own_rows(peer), :],
                dst_ref=ret.at[:, :, columns],
                send_sem=ret_send.at[mask - 1],
                recv_sem=ret_recv.at[mask - 1],
                device_id={"context": peer},
                device_id_type=MESH,
            ).start()
        ret[:, :, columns] = obuf[head, :, mine, :]
        return carry

    lax.fori_loop(0, heads, one_head, 0)

    for copy in mod_copies:
        copy.wait()
    chunk = math.gcd(quarter, width)
    for piece in range(3 * width // chunk):
        row, at = divmod(piece * chunk, width)
        owner, inside = divmod(piece * chunk, cols_w)
        part, off = divmod(inside, quarter)
        mods[row : row + 1, at : at + chunk] = (
            mod_r[owner, 2 * part : 2 * part + 1, off : off + chunk] + bm_ref[row : row + 1, at : at + chunk]
        )
        mods[row + 3 : row + 4, at : at + chunk] = mod_r[owner, 2 * part + 1 : 2 * part + 2, off : off + chunk]
    local[1].wait()
    local[2].wait()
    mods[2:3, :] = 1.0 + mods[2:3, :]

    for mask in masks:
        columns = pl.ds(pl.multiple_of(flip(me, mask) * (heads * HEAD), HEAD), heads * HEAD)
        theirs = ret.at[:, :, columns]
        pltpu.make_async_copy(theirs, theirs, ret_recv.at[mask - 1]).wait()

    lines = 16

    def norm(index, carry):
        rows = pl.ds(pl.multiple_of(index * lines, lines), lines)
        att = ret[0, rows, :].astype(jnp.float32)
        hidden = resv[0, rows, :].astype(jnp.float32) + mods[0:1, :] * att
        hidden_dot = (
            resv[1, rows, :].astype(jnp.float32)
            + mods[0:1, :] * ret[1, rows, :].astype(jnp.float32)
            + mods[3:4, :] * att
        )
        centered = hidden - jnp.mean(hidden, axis=1, keepdims=True)
        inverse = lax.rsqrt(jnp.mean(centered * centered, axis=1, keepdims=True) + EPS)
        unit = centered * inverse
        unit_dot = (
            hidden_dot
            - jnp.mean(hidden_dot, axis=1, keepdims=True)
            - unit * jnp.mean(unit * hidden_dot, axis=1, keepdims=True)
        ) * inverse
        outv[0, rows, :] = (unit * mods[2:3, :] + mods[1:2, :]).astype(jnp.bfloat16)
        outv[1, rows, :] = (unit_dot * mods[2:3, :] + unit * mods[5:6, :] + mods[4:5, :]).astype(jnp.bfloat16)
        pltpu.make_async_copy(outv.at[0, rows, :], out_ref.at[0, rows, :], out_sem.at[0]).start()
        pltpu.make_async_copy(outv.at[1, rows, :], outt_ref.at[0, rows, :], out_sem.at[1]).start()
        return carry

    lax.fori_loop(0, tokens // lines, norm, 0)

    for mask in masks:
        sent = rbuf.at[:, :, mine, :]
        pltpu.make_async_copy(sent, sent, in_send.at[mask - 1]).wait()
        sent = obuf.at[:, :, mine, :]
        pltpu.make_async_copy(sent, sent, ret_send.at[mask - 1]).wait()
    pltpu.make_async_copy(outv.at[0], out_ref.at[0], out_sem.at[0]).wait()
    pltpu.make_async_copy(outv.at[1], outt_ref.at[0], out_sem.at[1]).wait()


def on_device(n_ctx, n_dp, *arrays):
    res, q, tf, w = arrays[0], arrays[2], arrays[8], arrays[10]
    _, tokens, width = res.shape
    length = tokens * n_ctx
    heads = HEADS // n_ctx
    rows_w, cols_w = w.shape
    bf16, f32 = jnp.bfloat16, jnp.float32
    dma = pltpu.SemaphoreType.DMA
    anywhere = pl.BlockSpec(memory_space=pl.ANY)
    vmem = pl.BlockSpec(memory_space=pltpu.VMEM)
    return pl.pallas_call(
        functools.partial(kernel, n_ctx, n_dp),
        out_shape=(jax.ShapeDtypeStruct(res.shape, bf16),) * 2,
        in_specs=[anywhere] * 8 + [vmem, vmem, anywhere, vmem],
        out_specs=(anywhere,) * 2,
        scratch_shapes=[
            pltpu.VMEM((heads, 6, length, HEAD), bf16),
            pltpu.VMEM((heads, 2, length, HEAD), bf16),
            pltpu.VMEM((2, tokens, width), bf16),
            pltpu.VMEM((2, tokens, width), bf16),
            pltpu.VMEM((rows_w, cols_w), bf16),
            pltpu.VMEM((n_dp, 8, rows_w), f32),
            pltpu.VMEM((n_dp, 8, rows_w), f32),
            pltpu.VMEM((n_dp, 8, cols_w), f32),
            pltpu.VMEM((n_dp, 8, cols_w), f32),
            pltpu.VMEM((8, cols_w // 4), f32),
            pltpu.VMEM((n_ctx, 8, cols_w // 4), f32),
            pltpu.VMEM((8, width), f32),
            pltpu.VMEM((2, tokens, width), bf16),
            dma((n_ctx - 1,)),
            dma((heads, n_ctx - 1)),
            dma((heads,)),
            dma((n_ctx - 1,)),
            dma((n_ctx - 1,)),
            dma((n_dp - 1,)),
            dma((n_dp - 1,)),
            dma((n_dp - 1,)),
            dma((n_dp - 1,)),
            dma((n_ctx - 1,)),
            dma((n_ctx - 1,)),
            dma((3,)),
            dma((2,)),
        ],
        compiler_params=pltpu.CompilerParams(
            collective_id=0, has_side_effects=True, vmem_limit_bytes=56 * 1024 * 1024
        ),
    )(*arrays)


def solution(mesh):
    spec = P("dp", "context", None)
    return jax.shard_map(
        functools.partial(on_device, mesh.shape["context"], mesh.shape["dp"]),
        mesh=mesh,
        in_specs=(spec,) * 8 + (P("dp", None), P("dp", None), P("dp", "context"), P()),
        out_specs=(spec, spec),
        check_vma=False,
    )
```

```python
import functools
import math

import jax
import jax.numpy as jnp
from jax import lax
from jax.experimental import pallas as pl
from jax.experimental.pallas import tpu as pltpu
from jax.sharding import PartitionSpec as P

HEADS = 32
HEAD = 128
EPS = 1e-06
BLOCK = 32
MESH = pl.DeviceIdType.MESH


def flip(index, mask):
    bit = 1
    while bit <= mask:
        if mask & bit:
            index = index + bit * (1 - 2 * lax.rem(index // bit, 2))
        bit *= 2
    return index


def kernel(
    n_ctx,
    n_dp,
    res_ref,
    rest_ref,
    q_ref,
    k_ref,
    v_ref,
    dq_ref,
    dk_ref,
    dv_ref,
    tf_ref,
    tt_ref,
    w_ref,
    bm_ref,
    out_ref,
    outt_ref,
    rbuf,
    obuf,
    ret,
    resv,
    wv,
    act_s,
    act_r,
    part_s,
    part_r,
    mod_s,
    mod_r,
    mods,
    in_send,
    in_recv,
    own_sem,
    ret_send,
    ret_recv,
    late_send,
    late_recv,
    act_send,
    act_recv,
    part_send,
    part_recv,
    mod_send,
    mod_recv,
    loc_sem,
):
    heads, _, length, _ = rbuf.shape
    early = heads // 2
    tokens = ret.shape[1]
    width = ret.shape[2]
    rows_w, cols_w = wv.shape
    me = lax.axis_index("context")
    clip = lax.axis_index("dp")
    masks = list(range(n_ctx - 1, 0, -1))
    steps = list(range(1, n_dp))
    sources = (q_ref, k_ref, v_ref, dq_ref, dk_ref, dv_ref)

    barrier = pltpu.get_barrier_semaphore()
    for mask in masks:
        pl.semaphore_signal(barrier, inc=1, device_id={"context": flip(me, mask)}, device_id_type=MESH)
    for step in steps:
        pl.semaphore_signal(barrier, inc=1, device_id={"dp": lax.rem(clip + step, n_dp)}, device_id_type=MESH)

    local = [
        pltpu.make_async_copy(w_ref, wv, loc_sem.at[0]),
        pltpu.make_async_copy(res_ref.at[0], resv.at[0], loc_sem.at[1]),
        pltpu.make_async_copy(rest_ref.at[0], resv.at[1], loc_sem.at[2]),
    ]
    local[0].start()

    def own_rows(owner):
        return pl.ds(pl.multiple_of(owner * tokens, tokens), tokens)

    mine = own_rows(me)
    pl.semaphore_wait(barrier, len(masks) + len(steps))

    def send_head(head, carry):
        for mask in masks:
            peer = flip(me, mask)
            at = pl.multiple_of((peer * heads + head) * HEAD, HEAD)
            for slot, source in enumerate(sources):
                pltpu.make_async_remote_copy(
                    src_ref=source.at[0, :, pl.ds(at, HEAD)],
                    dst_ref=rbuf.at[head, slot, mine, :],
                    send_sem=in_send.at[mask - 1],
                    recv_sem=in_recv.at[head, mask - 1],
                    device_id={"context": peer},
                    device_id_type=MESH,
                ).start()
        return carry

    lax.fori_loop(0, heads, send_head, 0)

    def own_head(head, carry):
        at = pl.multiple_of((me * heads + head) * HEAD, HEAD)
        for slot, source in enumerate(sources):
            pltpu.make_async_copy(
                source.at[0, :, pl.ds(at, HEAD)], rbuf.at[head, slot, mine, :], own_sem.at[head]
            ).start()
        return carry

    x = tf_ref[...]
    gate = 1.0 / (1.0 + jnp.exp(-x))
    act = x * gate
    act_dot = tt_ref[...] * (gate * (1.0 + x * (1.0 - gate)))
    act_s[...] = jnp.zeros_like(act_s)
    for step in range(n_dp):
        act_s[step, 0:1, :] = act[:, step * rows_w : (step + 1) * rows_w]
        act_s[step, 1:2, :] = act_dot[:, step * rows_w : (step + 1) * rows_w]
    act_copies = []
    for step in steps:
        peer = lax.rem(clip + step, n_dp)
        copy = pltpu.make_async_remote_copy(
            src_ref=act_s.at[peer],
            dst_ref=act_r.at[clip],
            send_sem=act_send.at[step - 1],
            recv_sem=act_recv.at[step - 1],
            device_id={"dp": peer},
            device_id_type=MESH,
        )
        copy.start()
        act_copies.append(copy)
    lax.fori_loop(0, heads, own_head, 0)
    local[1].start()
    local[2].start()
    act_r[clip] = act_s[clip]
    for copy in act_copies:
        copy.wait()
    local[0].wait()
    lhs = act_r[...].reshape(n_dp * 8, rows_w).astype(jnp.bfloat16)
    tile = cols_w // 6

    for t in range(6):
        cols = slice(t * tile, (t + 1) * tile)
        prod = jnp.dot(lhs, wv[:, cols], preferred_element_type=jnp.float32)
        part_s[:, :, cols] = prod.reshape(n_dp, 8, tile)
    part_copies = []
    for step in steps:
        peer = lax.rem(clip + step, n_dp)
        copy = pltpu.make_async_remote_copy(
            src_ref=part_s.at[peer],
            dst_ref=part_r.at[clip],
            send_sem=part_send.at[step - 1],
            recv_sem=part_recv.at[step - 1],
            device_id={"dp": peer},
            device_id_type=MESH,
        )
        copy.start()
        part_copies.append(copy)
    part_r[clip] = part_s[clip]
    for copy in part_copies:
        copy.wait()
    total = part_r[0]
    for step in steps:
        total = total + part_r[step]
    quarter = cols_w // 4
    for piece in range(4):
        mod_s[2 * piece : 2 * piece + 2, :] = total[0:2, piece * quarter : (piece + 1) * quarter]
    mod_copies = []
    for mask in masks:
        copy = pltpu.make_async_remote_copy(
            src_ref=mod_s,
            dst_ref=mod_r.at[me],
            send_sem=mod_send.at[mask - 1],
            recv_sem=mod_recv.at[mask - 1],
            device_id={"context": flip(me, mask)},
            device_id_type=MESH,
        )
        copy.start()
        mod_copies.append(copy)
    mod_r[me] = mod_s[...]

    factor = 1.0 / HEAD**0.5
    block = min(256, length)

    def one_head(head, carry):
        pltpu.make_async_copy(rbuf.at[head, :, mine, :], rbuf.at[head, :, mine, :], own_sem.at[head]).wait()
        for mask in masks:
            theirs = rbuf.at[head, :, own_rows(flip(me, mask)), :]
            pltpu.make_async_copy(theirs, theirs, in_recv.at[head, mask - 1]).wait()

        here = pl.ds(pl.multiple_of(head * HEAD, HEAD), HEAD)

        def one_block(index, carry):
            rows = pl.ds(pl.multiple_of(index * block, block), block)
            query = rbuf[head, 0, rows, :]
            query_dot = rbuf[head, 3, rows, :]
            keyset = rbuf[head, 1]
            key_dot = rbuf[head, 4]
            values = rbuf[head, 2]
            value_dot = rbuf[head, 5]
            last = (((1,), (1,)), ((), ()))
            scores = lax.dot_general(query, keyset, last, preferred_element_type=jnp.float32) * factor
            score_dot = (
                lax.dot_general(
                    jnp.concatenate([query_dot, query], axis=1),
                    jnp.concatenate([keyset, key_dot], axis=1),
                    last,
                    preferred_element_type=jnp.float32,
                )
                * factor
            )
            top = jnp.max(scores, axis=1, keepdims=True)
            expo = jnp.exp(scores - top)
            probs = expo * (1.0 / jnp.sum(expo, axis=1, keepdims=True))
            probs_low = probs.astype(jnp.bfloat16)
            weighted = probs * score_dot
            centre = jnp.sum(weighted, axis=1, keepdims=True)
            weighted_low = weighted.astype(jnp.bfloat16)
            both = jnp.dot(
                probs_low, jnp.concatenate([values, value_dot], axis=1), preferred_element_type=jnp.float32
            )
            attended = both[:, :HEAD]
            tangent = (
                both[:, HEAD:]
                + jnp.dot(weighted_low, values, preferred_element_type=jnp.float32)
                - centre * attended
            )
            obuf[0, rows, here] = attended.astype(jnp.bfloat16)
            obuf[1, rows, here] = tangent.astype(jnp.bfloat16)
            return carry

        lax.fori_loop(0, length // block, one_block, 0)
        columns = pl.ds(pl.multiple_of((me * heads + head) * HEAD, HEAD), HEAD)

        @pl.when(head < early)
        def _():
            for mask in masks:
                peer = flip(me, mask)
                pltpu.make_async_remote_copy(
                    src_ref=obuf.at[:, own_rows(peer), here],
                    dst_ref=ret.at[:, :, columns],
                    send_sem=ret_send.at[mask - 1],
                    recv_sem=ret_recv.at[mask - 1],
                    device_id={"context": peer},
                    device_id_type=MESH,
                ).start()

        ret[:, :, columns] = obuf[:, mine, here]
        return carry

    lax.fori_loop(0, heads, one_head, 0)

    span = (heads - early) * HEAD
    late = pl.ds(early * HEAD, span)
    late_out = pl.ds(pl.multiple_of((me * heads + early) * HEAD, HEAD), span)
    blocks = tokens // BLOCK

    def send_block(index, carry):
        for mask in masks:
            peer = flip(me, mask)
            pltpu.make_async_remote_copy(
                src_ref=obuf.at[:, pl.ds(pl.multiple_of(peer * tokens + index * BLOCK, BLOCK), BLOCK), late],
                dst_ref=ret.at[:, pl.ds(pl.multiple_of(index * BLOCK, BLOCK), BLOCK), late_out],
                send_sem=late_send.at[mask - 1],
                recv_sem=late_recv.at[index, mask - 1],
                device_id={"context": peer},
                device_id_type=MESH,
            ).start()
        return carry

    lax.fori_loop(0, blocks, send_block, 0)

    for copy in mod_copies:
        copy.wait()
    chunk = math.gcd(quarter, width)
    for piece in range(3 * width // chunk):
        row, at = divmod(piece * chunk, width)
        owner, inside = divmod(piece * chunk, cols_w)
        part, off = divmod(inside, quarter)
        mods[row : row + 1, at : at + chunk] = (
            mod_r[owner, 2 * part : 2 * part + 1, off : off + chunk] + bm_ref[row : row + 1, at : at + chunk]
        )
        mods[row + 3 : row + 4, at : at + chunk] = mod_r[owner, 2 * part + 1 : 2 * part + 2, off : off + chunk]
    local[1].wait()
    local[2].wait()
    mods[2:3, :] = 1.0 + mods[2:3, :]

    for mask in masks:
        columns = pl.ds(pl.multiple_of(flip(me, mask) * (heads * HEAD), HEAD), early * HEAD)
        theirs = ret.at[:, :, columns]
        pltpu.make_async_copy(theirs, theirs, ret_recv.at[mask - 1]).wait()

    lines = 16

    def norm(index, carry):
        rows = pl.ds(pl.multiple_of(index * lines, lines), lines)
        att = ret[0, rows, :].astype(jnp.float32)
        hidden = resv[0, rows, :].astype(jnp.float32) + mods[0:1, :] * att
        hidden_dot = (
            resv[1, rows, :].astype(jnp.float32)
            + mods[0:1, :] * ret[1, rows, :].astype(jnp.float32)
            + mods[3:4, :] * att
        )
        centered = hidden - jnp.mean(hidden, axis=1, keepdims=True)
        inverse = lax.rsqrt(jnp.mean(centered * centered, axis=1, keepdims=True) + EPS)
        unit = centered * inverse
        unit_dot = (
            hidden_dot
            - jnp.mean(hidden_dot, axis=1, keepdims=True)
            - unit * jnp.mean(unit * hidden_dot, axis=1, keepdims=True)
        ) * inverse
        out_ref[0, rows, :] = (unit * mods[2:3, :] + mods[1:2, :]).astype(jnp.bfloat16)
        outt_ref[0, rows, :] = (unit_dot * mods[2:3, :] + unit * mods[5:6, :] + mods[4:5, :]).astype(jnp.bfloat16)
        return carry

    def norm_block(index, carry):
        for mask in masks:
            columns = pl.ds(pl.multiple_of((flip(me, mask) * heads + early) * HEAD, HEAD), span)
            theirs = ret.at[:, pl.ds(pl.multiple_of(index * BLOCK, BLOCK), BLOCK), columns]
            pltpu.make_async_copy(theirs, theirs, late_recv.at[index, mask - 1]).wait()
        lax.fori_loop(index * (BLOCK // lines), (index + 1) * (BLOCK // lines), norm, 0)
        return carry

    lax.fori_loop(0, blocks, norm_block, 0)

    for mask in masks:
        sent = rbuf.at[:, :, mine, :]
        pltpu.make_async_copy(sent, sent, in_send.at[mask - 1]).wait()
        sent = obuf.at[:, mine, pl.ds(0, early * HEAD)]
        pltpu.make_async_copy(sent, sent, ret_send.at[mask - 1]).wait()
        sent = obuf.at[:, mine, late]
        pltpu.make_async_copy(sent, sent, late_send.at[mask - 1]).wait()


def on_device(n_ctx, n_dp, *arrays):
    res, q, tf, w = arrays[0], arrays[2], arrays[8], arrays[10]
    _, tokens, width = res.shape
    length = tokens * n_ctx
    heads = HEADS // n_ctx
    rows_w, cols_w = w.shape
    bf16, f32 = jnp.bfloat16, jnp.float32
    dma = pltpu.SemaphoreType.DMA
    anywhere = pl.BlockSpec(memory_space=pl.ANY)
    vmem = pl.BlockSpec(memory_space=pltpu.VMEM)
    return pl.pallas_call(
        functools.partial(kernel, n_ctx, n_dp),
        out_shape=(jax.ShapeDtypeStruct(res.shape, bf16),) * 2,
        in_specs=[anywhere] * 8 + [vmem, vmem, anywhere, vmem],
        out_specs=(vmem,) * 2,
        scratch_shapes=[
            pltpu.VMEM((heads, 6, length, HEAD), bf16),
            pltpu.VMEM((2, length, heads * HEAD), bf16),
            pltpu.VMEM((2, tokens, width), bf16),
            pltpu.VMEM((2, tokens, width), bf16),
            pltpu.VMEM((rows_w, cols_w), bf16),
            pltpu.VMEM((n_dp, 8, rows_w), f32),
            pltpu.VMEM((n_dp, 8, rows_w), f32),
            pltpu.VMEM((n_dp, 8, cols_w), f32),
            pltpu.VMEM((n_dp, 8, cols_w), f32),
            pltpu.VMEM((8, cols_w // 4), f32),
            pltpu.VMEM((n_ctx, 8, cols_w // 4), f32),
            pltpu.VMEM((8, width), f32),
            dma((n_ctx - 1,)),
            dma((heads, n_ctx - 1)),
            dma((heads,)),
            dma((n_ctx - 1,)),
            dma((n_ctx - 1,)),
            dma((n_ctx - 1,)),
            dma((tokens // BLOCK, n_ctx - 1)),
            dma((n_dp - 1,)),
            dma((n_dp - 1,)),
            dma((n_dp - 1,)),
            dma((n_dp - 1,)),
            dma((n_ctx - 1,)),
            dma((n_ctx - 1,)),
            dma((3,)),
        ],
        compiler_params=pltpu.CompilerParams(
            collective_id=0, has_side_effects=True, vmem_limit_bytes=40 * 1024 * 1024
        ),
    )(*(pltpu.with_memory_space_constraint(a, pltpu.HBM) for a in arrays))


def solution(mesh):
    spec = P("dp", "context", None)
    return jax.shard_map(
        functools.partial(on_device, mesh.shape["context"], mesh.shape["dp"]),
        mesh=mesh,
        in_specs=(spec,) * 8 + (P("dp", None), P("dp", None), P("dp", "context"), P()),
        out_specs=(spec, spec),
        check_vma=False,
    )
```
